32 devices in a mesh: gx: 4 (over z), gy: 4 (over x, core), gz: 2 (over y).
Axes of the slice: x: 2, y: 2, z: 4, core: 2. Of those that a mesh axis runs over, the one named last changes fastest.
Arguments:
- populations: float32 [19, 16, 128, 512], P(None, 'gz', 'gy', 'gx'), as said below
- rbf_weights: bfloat16 [2048, 128, 128], P(('gx', 'gy', 'gz')), may hold values from -0.5 to 0.5
- owner_map: int32 [2048, 1], P(('gx', 'gy', 'gz')), may hold values from 0 to 7; in each aligned block of 64 rows (0 to 63, 64 to 127, ...) at most 16 rows name the same one
- shell_slot: int32 [2048, 1], P(('gx', 'gy', 'gz')), may hold values from 0 to 7
- compliance: float32 [256, 128, 128], P(('gx', 'gy', 'gz')), may hold values from -0.5 to 0.5
- neighbour_compliance: float32 [4096, 128], P(('gx', 'gy', 'gz')), may hold values from -0.5 to 0.5
- interface_row: int32 [2048], P(('gx', 'gy', 'gz')), may hold values from 0 to 255, as said below
Outputs:
- new_populations: float32 [19, 16, 128, 512], P(None, 'gz', 'gy', 'gx')
- displacement: float32 [256, 3, 128], P(('gx', 'gy', 'gz'))
- wall_motion: float32 [2048, 3, 128], P(('gx', 'gy', 'gz'))
The draws below stay inside these ranges and needn't reach their ends.
Inputs may be any that keep to these rules, and one draw needn't show every extreme that they name: `populations`: each population lies between 0.5 and 1.5 times its lattice weight. `owner_map`: among the 64 rows of one device no owner appears more than 16 times, and some owner appears exactly 16 times. `interface_row`: the 64 rows of one device are distinct.
All inputs are finite; a program needn't handle non-finite values.
Results may differ from the reference program's by a relative error of at most 0.004.
Values sent between devices are 32-bit elements; how exact they have to be, the bound alone decides.
A program may use at most 64 MiB of HBM per device.

```python
import math
import jax
import jax.numpy as jnp
import numpy as np
from jax import lax

CX = 128
CY = 32
CZ = 8
NB = 64
SB = 8
SN = 128
CAP = 16
NX = 512
NY = 128
NZ = 16
INTERFACE = 2048
SHELL_BLOCKS = 256
N_GX = 4
N_GY = 4
N_GZ = 2
DEVICES = 32


lattice_weight = (1.0 / 3.0,) + (1.0 / 18.0,) * 6 + (1.0 / 36.0,) * 12


def draw_populations(key, part):
    weights = jnp.array(lattice_weight, dtype=jnp.float32)
    factor = jax.random.uniform(key, (19, NZ, NY, NX), jnp.float32, 0.5, 1.5)
    return weights[:, None, None, None] * factor


def pick_rows(device_key):
    return jax.random.permutation(device_key, CZ * CY)[:NB]


def draw_interface_row(key, part):
    device_keys = jax.random.split(jax.random.fold_in(key, 23), INTERFACE // NB)
    chosen = jax.vmap(pick_rows)(device_keys)
    return chosen.reshape(INTERFACE).astype(jnp.int32)


def plant(result, key, low, high):
    place = [jax.random.randint(jax.random.fold_in(key, axis), (), 0, length) for axis, length in enumerate(result.shape)]
    widest = result.shape.index(max(result.shape))
    beside = place[:widest] + [(place[widest] + 1) % result.shape[widest]] + place[widest + 1:]
    return result.at[tuple(place)].set(low).at[tuple(beside)].set(high)


def levels(own_key, dims, cuts, smallest, high):
    def one(dim, shards_of):
        heights = jax.random.uniform(jax.random.fold_in(jax.random.fold_in(own_key, 6), dim), (shards_of,), jnp.float32, smallest / len(cuts), high / len(cuts))
        return jnp.repeat(jnp.exp(heights), dims[dim] // shards_of).reshape((-1,) + (1,) * (len(dims) - dim - 1))

    level = one(*cuts[0])
    for cut in cuts[1:]:
        level = level * one(*cut)
    return level


def routed_block(key, own, number, rows, count, top, limit, skew):
    ranking = jax.random.permutation(key, count)
    heavy_load, ordinary = load_shares(count, rows * top, limit, skew, True), load_shares(count, rows * top, limit, skew, False)
    places = jnp.arange(count)

    def named(sizes, offset_by):
        used = int((sizes > 0).sum())
        fixed = max(1, used // 4)
        moved = fixed + (places - fixed + offset_by * (used - fixed)) % max(1, count - fixed)
        return jnp.zeros((count,), jnp.int32).at[ranking[jnp.where(places < fixed, places, moved)]].set(jnp.asarray(sizes, jnp.int32))

    sizes = jnp.where(number % 4 == 0, named(heavy_load, number // 4), named(ordinary, number - number // 4 - 1))
    mixed = jax.random.permutation(jax.random.fold_in(own, 3), count)
    source_of, receiver = mixed[0:count // 2 * 2:2], mixed[1:count // 2 * 2:2]
    room = jnp.minimum(sizes[source_of] - 1, limit - sizes[receiver]) // 2
    room = jnp.where((source_of == ranking[0]) | (receiver == ranking[0]) | (sizes[receiver] == 0), 0, jnp.maximum(room, 0))
    moved = jax.random.randint(jax.random.fold_in(own, 4), (count // 2,), 0, 1 << 20) % (room + 1)
    sizes = sizes.at[source_of].add(-moved).at[receiver].add(moved)
    labels = jnp.searchsorted(jnp.cumsum(sizes), jnp.arange(rows * top), side="right").astype(jnp.int32)
    table = labels.reshape(top, rows).T
    table = table[jax.random.permutation(jax.random.fold_in(own, 1), rows)]
    offset_by = jax.random.randint(jax.random.fold_in(own, 2), (rows, 1), 0, top)
    return jnp.take_along_axis(table, (jnp.arange(top)[None, :] + offset_by) % top, axis=1)


def load_shares(count, total, limit, lean, full):
    portions = [(1 << 20) // math.isqrt(standing ** lean) + 1 for standing in range(1, count + 1)]
    largest = limit if full else min(limit, max(-(-total // count), total * portions[0] // sum(portions)))
    least = 1 if total - largest >= count - 1 else 0
    counts, rest = [largest] + [least] * (count - 1), total - largest - least * (count - 1)
    while rest > 0:
        free = [i for i in range(1, count) if counts[i] < largest] or [i for i in range(1, count) if counts[i] < limit]
        whole, budget = sum([portions[i] for i in free]), rest
        for i in free:
            more = min(limit - counts[i], max(1, budget * portions[i] // whole), rest)
            counts[i] = counts[i] + more
            rest = rest - more
    return np.array(counts)


def bell_draw(key, shape, deviation, bound, cuts=(), held_as=jnp.bfloat16):
    result = deviation * jax.random.normal(key, shape, jnp.float32)
    if cuts:
        result = result * levels(key, shape, cuts, -0.22, 0.18)
    return jnp.clip(result, -bound, bound).astype(held_as)


def setup_inputs(seed: int = 0) -> dict:
    streams_of = jax.random.split(jax.random.key(seed), 8)
    populations = draw_populations(jax.random.fold_in(streams_of[7], 71), 0)
    rbf_weights = bell_draw(streams_of[1], (INTERFACE, CX, SN), CX ** -0.5, 0.5, ((0, 32),))
    owner_map_keys = jax.random.split(jax.random.fold_in(streams_of[2], 1), INTERFACE // NB)
    owner_map_turns = jax.random.permutation(jax.random.fold_in(streams_of[2], 3), INTERFACE // NB)
    owner_map = jax.vmap(lambda own, number: routed_block(jax.random.fold_in(streams_of[2], 2), own, number, NB, N_GY * N_GZ, 1, CAP, 2))(owner_map_keys, owner_map_turns).reshape((INTERFACE, 1))
    shell_slot = plant(jax.random.randint(streams_of[3], (INTERFACE, 1), 0, SB), jax.random.fold_in(streams_of[3], 1), 0, SB - 1).astype(jnp.int32)
    compliance = bell_draw(streams_of[4], (SHELL_BLOCKS, SN, SN), SN ** -0.5, 0.5, ((0, 32),), jnp.float32)
    neighbour_compliance = bell_draw(streams_of[5], (DEVICES * SN, SN), SN ** -0.5, 0.5, ((0, 32),), jnp.float32)
    interface_row = draw_interface_row(jax.random.fold_in(streams_of[7], 71), 0)
    return {"populations": populations, "rbf_weights": rbf_weights, "owner_map": owner_map, "shell_slot": shell_slot, "compliance": compliance, "neighbour_compliance": neighbour_compliance, "interface_row": interface_row}


lattice_velocity = ((0, 0, 0), (1, 0, 0), (-1, 0, 0), (0, 1, 0), (0, -1, 0), (0, 0, 1), (0, 0, -1),
                    (1, 1, 0), (-1, -1, 0), (1, -1, 0), (-1, 1, 0), (1, 0, 1), (-1, 0, -1), (1, 0, -1),
                    (-1, 0, 1), (0, 1, 1), (0, -1, -1), (0, 1, -1), (0, -1, 1))
lattice_weight = (1.0 / 3.0,) + (1.0 / 18.0,) * 6 + (1.0 / 36.0,) * 12
load_scale = 30.0
relaxation = 1.6


def moment_matrix():
    return jnp.array([[1.0] * 19,
                      [float(item[0]) for item in lattice_velocity],
                      [float(item[1]) for item in lattice_velocity],
                      [float(item[2]) for item in lattice_velocity]], dtype=jnp.float32)


def collide(flattened):
    moments = jnp.dot(moment_matrix(), flattened, precision=lax.Precision.HIGHEST)
    density = moments[0]
    velocity = moments[1:4] / density
    speed_square = velocity[0] * velocity[0] + velocity[1] * velocity[1] + velocity[2] * velocity[2]
    relaxed = []
    for direction in range(19):
        along_x, along_y, along_z = lattice_velocity[direction]
        projected = along_x * velocity[0] + along_y * velocity[1] + along_z * velocity[2]
        equilibrium = lattice_weight[direction] * density * (
            1.0 + 3.0 * projected + 4.5 * projected * projected - 1.5 * speed_square)
        relaxed.append(flattened[direction] - relaxation * (flattened[direction] - equilibrium))
    return relaxed, moments


def block_forces(pair):
    traction, weights = pair
    return jnp.einsum('bkc,bcs->bks', traction.astype(jnp.float32), weights.astype(jnp.float32),
                      precision=lax.Precision.HIGHEST)


def block_motion(pair):
    returned, weights = pair
    return jnp.einsum('bks,bcs->bkc', returned.astype(jnp.float32), weights.astype(jnp.float32),
                      precision=lax.Precision.HIGHEST)


def reference(populations, rbf_weights, owner_map, shell_slot, compliance, neighbour_compliance, interface_row):
    grid_shape = populations.shape[1:]
    relaxed, moments = collide(populations.reshape(19, -1))
    passed = []
    for direction in range(19):
        along_x, along_y, along_z = lattice_velocity[direction]
        passed.append(jnp.roll(relaxed[direction].reshape(grid_shape), (along_z, along_y, along_x), axis=(0, 1, 2)))
    new_populations = jnp.stack(passed)

    owner_count = N_GY * N_GZ
    devices = INTERFACE // NB
    device_index = jnp.arange(INTERFACE, dtype=jnp.int32) // NB
    slab_index = device_index // owner_count
    pencil_index = (device_index // N_GZ) % N_GY
    block_index = device_index % N_GZ
    cell_z = block_index * CZ + interface_row // CY
    cell_y = pencil_index * CY + interface_row % CY
    momentum = moments[1:4].reshape(3, NZ, NY, N_GX, CX)
    interface_momentum = jnp.transpose(momentum[:, cell_z, cell_y, slab_index, :], (1, 0, 2))
    traction = (load_scale * interface_momentum).astype(jnp.bfloat16)
    forces = lax.map(block_forces, (traction.reshape(devices, NB, 3, CX),
                                    rbf_weights.reshape(devices, NB, CX, SN)))
    forces = forces.reshape(INTERFACE, 3 * SN)

    target = ((slab_index * owner_count + owner_map[:, 0]) * SB + shell_slot[:, 0]).astype(jnp.int32)
    loads = jax.ops.segment_sum(forces, target, num_segments=SHELL_BLOCKS).reshape(SHELL_BLOCKS, 3, SN)
    displacement = jnp.einsum('skn,snm->skm', loads, compliance, precision=lax.Precision.HIGHEST)
    last_loads = loads.reshape(devices, SB, 3, SN)[:, SB - 1]
    previous = jnp.concatenate([jnp.zeros((1, 3, SN), jnp.float32), last_loads[:-1]], 0)
    has_left = (jnp.arange(devices, dtype=jnp.int32) % owner_count > 0).astype(jnp.float32)
    shared_term = jnp.einsum('dkn,dnm->dkm', previous, neighbour_compliance.reshape(devices, SN, SN),
                             precision=lax.Precision.HIGHEST) * has_left[:, None, None]
    displacement = displacement.reshape(devices, SB, 3, SN).at[:, 0].add(shared_term).reshape(SHELL_BLOCKS, 3, SN)

    returned = displacement[target].astype(jnp.bfloat16)
    wall_motion = lax.map(block_motion, (returned.reshape(devices, NB, 3, SN),
                                         rbf_weights.reshape(devices, NB, CX, SN)))
    return new_populations, displacement, wall_motion.reshape(INTERFACE, 3, CX)
```

```python
import functools

import jax
import jax.numpy as jnp
from jax import lax
from jax.experimental import pallas as pl
from jax.experimental.pallas import tpu as pltpu
from jax.sharding import PartitionSpec as P

MESH = pl.DeviceIdType.MESH
F32 = jnp.float32
BF16 = jnp.bfloat16
I32 = jnp.int32

lattice_velocity = (
    (0, 0, 0),
    (1, 0, 0),
    (-1, 0, 0),
    (0, 1, 0),
    (0, -1, 0),
    (0, 0, 1),
    (0, 0, -1),
    (1, 1, 0),
    (-1, -1, 0),
    (1, -1, 0),
    (-1, 1, 0),
    (1, 0, 1),
    (-1, 0, -1),
    (1, 0, -1),
    (-1, 0, 1),
    (0, 1, 1),
    (0, -1, -1),
    (0, 1, -1),
    (0, -1, 1),
)
lattice_weight = (1.0 / 3.0,) + (1.0 / 18.0,) * 6 + (1.0 / 36.0,) * 12
load_scale = 30.0
relaxation = 1.6


def moving(component, sign):
    return [q for q in range(19) if lattice_velocity[q][component] == sign]


XP, XM = moving(0, 1), moving(0, -1)
YP, YM = moving(1, 1), moving(1, -1)
ZP, ZM = moving(2, 1), moving(2, -1)
NOT_Z = [q for q in range(19) if lattice_velocity[q][2] == 0]


def iota(shape, dim):
    return lax.broadcasted_iota(I32, shape, dim)


def split(value):
    high = value.astype(BF16)
    low = (value - high.astype(F32)).astype(BF16)
    return high, low


def dot(a, b):
    return jnp.dot(a, b, preferred_element_type=F32)


def kernel(
    sizes,
    pop, rbf, owner, slot, comp, ncomp, row,
    out, disp, wall,
    f, moments, grid, mom, weights, compliance, coupling,
    gather, place, spread, traction, forces, part, recv, mine, shells,
    xs, xr, ys, yr, zr,
    in_sem, w_sem, ps_sem, pr_sem, ds_sem, dr_sem, hs_sem, hr_sem, zs_sem, zr_sem, o_sem,
):
    gxn, gyn, gzn = sizes
    owners = gyn * gzn
    depth, height, width = grid.shape[1:]
    blocks = weights.shape[0]
    shell = compliance.shape[0]
    rows8 = blocks * 8
    cells = depth * height
    gx, gy, gz = lax.axis_index("gx"), lax.axis_index("gy"), lax.axis_index("gz")
    me = gy * gzn + gz

    def peer(index):
        return (gx, index // gzn, index % gzn)

    def step(a, n, by):
        return lax.rem(a + by + n, n)

    right = (step(gx, gxn, 1), gy, gz)
    left = (step(gx, gxn, -1), gy, gz)
    north = (gx, step(gy, gyn, 1), gz)
    south = (gx, step(gy, gyn, -1), gz)
    up = (gx, gy, step(gz, gzn, 1))
    down = (gx, gy, step(gz, gzn, -1))

    loads_in = [pltpu.make_async_copy(pop.at[:, z], f.at[:, z], in_sem.at[z]) for z in range(depth)]
    for copy in loads_in:
        copy.start()
    fixed = [
        pltpu.make_async_copy(rbf, weights, w_sem.at[0]),
        pltpu.make_async_copy(comp, compliance, w_sem.at[1]),
        pltpu.make_async_copy(ncomp, coupling, w_sem.at[2]),
    ]
    for copy in fixed:
        copy.start()

    barrier = pltpu.get_barrier_semaphore()

    def greet(d, carry):
        pl.semaphore_signal(
            barrier, inc=1, device_id=peer(lax.rem(me + d, owners)), device_id_type=MESH
        )
        return carry

    lax.fori_loop(1, owners, greet, 0)
    for item in (left, right):
        pl.semaphore_signal(barrier, inc=1, device_id=item, device_id_type=MESH)

    square = iota((blocks, blocks), 0) == iota((blocks, blocks), 1)

    def down_rows(ref):
        return jnp.sum(jnp.where(square, ref[...], 0).astype(F32), axis=1, keepdims=True)

    row_s, owner_s, slot_s = down_rows(row), down_rows(owner), down_rows(slot)
    wide = jnp.concatenate(
        [jnp.broadcast_to(item, (blocks, 128)) for item in (row_s, owner_s, slot_s)], axis=1
    ).astype(BF16)
    repeat = (iota((rows8, blocks), 0) // 8 == iota((rows8, blocks), 1)).astype(F32).astype(BF16)
    tall = dot(repeat, wide).astype(I32)
    kind = iota((rows8, 128), 0) % 8
    row_key = tall[:, :128] + kind * cells
    lane = iota((rows8, 128), 1)
    for j in range(3 * cells // 128):
        hit = row_key == lane + 128 * j
        gather[:, j * 128 : (j + 1) * 128] = hit.astype(F32).astype(BF16)
    target_key = (tall[:, 128:256] * shell + tall[:, 256:]) * 3 + kind
    target_key = jnp.where(kind < 3, target_key, -2)
    for j in range(owners * 32 // 128):
        column = lane + 128 * j
        column_key = jnp.where(column % 32 < 3 * shell, column // 32 * (3 * shell) + column % 32, -1)
        spread[:, j * 128 : (j + 1) * 128] = (target_key == column_key).astype(F32).astype(BF16)
    target_s = ((owner_s * shell + slot_s) * 3).astype(I32)
    across = iota((blocks, rows8), 1)
    lane_key = jnp.sum(
        jnp.where(across // 8 == iota((blocks, rows8), 0), target_s, 0).astype(F32),
        axis=0, keepdims=True,
    ).astype(I32)
    lane_kind = iota((1, rows8), 1) % 8
    lane_key = jnp.where(lane_kind < 3, lane_key + lane_kind, -100)
    place_row = iota((owners * 32, rows8), 0)
    place_key = jnp.where(
        place_row % 32 < 3 * shell + 3,
        place_row // 32 * (3 * shell) - 3 + place_row % 32,
        -1000,
    )
    place[...] = (place_key == lane_key).astype(F32).astype(BF16)

    for z in range(depth):
        loads_in[z].wait()

        def moment(c, carry, z=z):
            at = pl.ds(pl.multiple_of(c * 16, 16), 16)
            v = [f[q, z, at, :] for q in range(19)]
            total = v[0]
            for q in range(1, 19):
                total = total + v[q]
            moments[0, z, at, :] = total
            for k in range(3):
                plus, minus = moving(k, 1), moving(k, -1)
                a, b = v[plus[0]], v[minus[0]]
                for q in plus[1:]:
                    a = a + v[q]
                for q in minus[1:]:
                    b = b + v[q]
                m = a - b
                moments[1 + k, z, at, :] = m
                here = pl.ds(pl.multiple_of(k * cells + z * height + c * 16, 16), 16)
                mom[here, :] = (load_scale * m).astype(BF16)
            return carry

        for c in range(height // 16):
            moment(c, 0)

    traction[...] = dot(gather[...], mom[...])
    fixed[0].wait()

    def force(g, carry):
        for i in range(8):
            at = pl.ds(pl.multiple_of(g * 64 + i * 8, 8), 8)
            forces[at, :] = dot(traction[at, :].astype(BF16), weights[g * 8 + i])
        return carry

    lax.fori_loop(0, blocks // 8, force, 0)
    high, low = split(forces[...])
    both = dot(place[...], jnp.concatenate([high, low], axis=1))
    part[...] = (both[:, :128] + both[:, 128:]).reshape(owners, 32, 128)
    pl.semaphore_wait(barrier, owners - 1 + 2)

    def part_copy(other, mine_at):
        return pltpu.make_async_remote_copy(
            src_ref=part.at[other], dst_ref=recv.at[mine_at],
            send_sem=ps_sem.at[other], recv_sem=pr_sem.at[mine_at],
            device_id=peer(other), device_id_type=MESH,
        )

    def send_part(d, carry):
        part_copy(lax.rem(me + d, owners), me).start()
        return carry

    lax.fori_loop(1, owners, send_part, 0)

    lanes = iota((16, width), 1)

    def collide(z, carry):
        for c in range(height // 16):
            at = pl.ds(c * 16, 16)
            rho = moments[0, z, at, :]
            inverse = 1.0 / rho
            u = [moments[1 + k, z, at, :] * inverse for k in range(3)]
            base = 1.0 - 1.5 * (u[0] * u[0] + u[1] * u[1] + u[2] * u[2])
            scaled = [relaxation * w * rho for w in (1 / 3.0, 1 / 18.0, 1 / 36.0)]
            result = [None] * 19
            result[0] = (1.0 - relaxation) * f[0, z, at, :] + scaled[0] * base
            for q in range(1, 19, 2):
                p = None
                for k in range(3):
                    s = lattice_velocity[q][k]
                    if s:
                        term = u[k]
                        p = (term if s > 0 else -term) if p is None else (p + term if s > 0 else p - term)
                w = scaled[1] if q < 7 else scaled[2]
                even = w * (base + 4.5 * (p * p))
                odd = w * (3.0 * p)
                result[q] = (1.0 - relaxation) * f[q, z, at, :] + (even + odd)
                result[q + 1] = (1.0 - relaxation) * f[q + 1, z, at, :] + (even - odd)
            sent = [xs[0, at, :], xs[1, at, :]]
            for d in range(5):
                here = lanes == d * depth + z
                sent[0] = jnp.where(here, result[XP[d]][:, width - 1 :], sent[0])
                sent[1] = jnp.where(here, result[XM[d]][:, :1], sent[1])
                result[XP[d]] = pltpu.roll(result[XP[d]], 1, 1)
                result[XM[d]] = pltpu.roll(result[XM[d]], width - 1, 1)
            xs[0, at, :] = sent[0]
            xs[1, at, :] = sent[1]
            for q in range(19):
                grid[q, z, at, :] = result[q]
        return carry

    xs[...] = jnp.zeros_like(xs)
    lax.fori_loop(0, depth, collide, 0)

    def halo(src, dst, number, device):
        return pltpu.make_async_remote_copy(
            src_ref=src, dst_ref=dst, send_sem=hs_sem.at[number], recv_sem=hr_sem.at[number],
            device_id=device, device_id_type=MESH,
        )

    x_copies = [halo(xs.at[0], xr.at[0], 0, right), halo(xs.at[1], xr.at[1], 1, left)]
    for copy in x_copies:
        copy.start()

    fixed[1].wait()
    fixed[2].wait()
    comp_high, comp_low = split(compliance[...])
    coup_high, coup_low = split(coupling[...])

    def take_part(d, total):
        other = lax.rem(me + d, owners)
        part_copy(me, other).wait_recv()
        return total + recv[other]

    load = lax.fori_loop(1, owners, take_part, part[me])
    load_high, load_low = split(load)
    aligned = 8 * (shell + 1)
    r8, c8 = iota((aligned, 32), 0), iota((aligned, 32), 1)
    expand = ((r8 % 8 < 3) & (r8 // 8 * 3 + r8 % 8 == c8)).astype(F32).astype(BF16)
    tall_load = dot(expand, jnp.concatenate([load_high, load_low], axis=1))
    moved = []
    for s in range(shell + 1):
        hi = tall_load[s * 8 : s * 8 + 8, :128]
        lo = tall_load[s * 8 : s * 8 + 8, 128:]
        pair = jnp.concatenate([hi, lo], axis=0).astype(BF16)
        first = comp_high[s - 1] if s else coup_high
        second = comp_low[s - 1] if s else coup_low
        a = dot(pair, first)
        b = dot(pair, second)
        moved.append(a[:8] + a[8:] + b[:8])
    moved[1] = moved[1] + moved[0]
    for s in range(shell):
        disp[s] = moved[s + 1][:3]
    r8, c8 = iota((32, 8 * shell), 0), iota((32, 8 * shell), 1)
    compact = ((c8 % 8 < 3) & (c8 // 8 * 3 + c8 % 8 == r8)).astype(F32).astype(BF16)
    rounded = jnp.concatenate(moved[1:], axis=0).astype(BF16)
    own = dot(compact, rounded)
    mine[...] = own
    shells[me] = own

    def disp_copy(other, at):
        return pltpu.make_async_remote_copy(
            src_ref=mine, dst_ref=shells.at[at],
            send_sem=ds_sem.at[other], recv_sem=dr_sem.at[at],
            device_id=peer(other), device_id_type=MESH,
        )

    def send_disp(d, carry):
        disp_copy(lax.rem(me + d, owners), me).start()
        return carry

    lax.fori_loop(1, owners, send_disp, 0)

    for copy in x_copies:
        copy.wait_recv()
    for d in range(5):
        for z in range(depth):
            i = d * depth + z
            grid[XP[d], z, :, 0:1] = xr[0, :, i : i + 1]
            grid[XM[d], z, :, width - 1 :] = xr[1, :, i : i + 1]
    for d in range(5):
        ys[0, d] = grid[YP[d], :, height - 1, :]
        ys[1, d] = grid[YM[d], :, 0, :]
    y_copies = [halo(ys.at[0], yr.at[0], 2, north), halo(ys.at[1], yr.at[1], 3, south)]
    for copy in y_copies:
        copy.start()
    ylane = iota((height, width), 0)

    for copy in y_copies:
        copy.wait_recv()

    def shift_y(z, carry):
        for d in range(5):
            q = YP[d]
            grid[q, z] = jnp.where(ylane == 0, yr[0, d, pl.ds(z, 1), :], pltpu.roll(grid[q, z], 1, 0))
            q = YM[d]
            grid[q, z] = jnp.where(
                ylane == height - 1, yr[1, d, pl.ds(z, 1), :], pltpu.roll(grid[q, z], height - 1, 0)
            )
        return carry

    lax.fori_loop(0, depth, shift_y, 0)
    z_copies = []
    for d in range(5):
        for side, q, z, device in ((0, ZP[d], depth - 1, up), (1, ZM[d], 0, down)):
            z_copies.append(
                pltpu.make_async_remote_copy(
                    src_ref=grid.at[q, z], dst_ref=zr.at[side, d],
                    send_sem=zs_sem.at[side, d], recv_sem=zr_sem.at[side, d],
                    device_id=device, device_id_type=MESH,
                )
            )
            z_copies[-1].start()
    written = []

    def write(src, dst):
        written.append(pltpu.make_async_copy(src, dst, o_sem.at[len(written)]))
        written[-1].start()

    for q in NOT_Z:
        write(grid.at[q], out.at[q])
    for d in range(5):
        write(grid.at[ZP[d], 0 : depth - 1], out.at[ZP[d], 1:depth])
        write(grid.at[ZM[d], 1:depth], out.at[ZM[d], 0 : depth - 1])

    def take_disp(d, carry):
        other = lax.rem(me + d, owners)
        disp_copy(other, other).wait_recv()
        return carry

    lax.fori_loop(1, owners, take_disp, 0)
    everything = shells[...].reshape(owners * 32, 128).astype(BF16)
    traction[...] = dot(spread[...], everything)

    def motion(g, carry):
        for i in range(8):
            at = pl.ds(pl.multiple_of(g * 64 + i * 8, 8), 8)
            value = lax.dot_general(
                traction[at, :].astype(BF16), weights[g * 8 + i],
                (((1,), (1,)), ((), ())), preferred_element_type=F32,
            )
            wall[g * 8 + i] = value[:3]
        return carry

    lax.fori_loop(0, blocks // 8, motion, 0)

    for copy in z_copies:
        copy.wait_recv()
    for d in range(5):
        write(zr.at[0, d], out.at[ZP[d], 0])
        write(zr.at[1, d], out.at[ZM[d], depth - 1])

    def drain(d, carry):
        other = lax.rem(me + d, owners)
        part_copy(other, me).wait_send()
        disp_copy(other, me).wait_send()
        return carry

    lax.fori_loop(1, owners, drain, 0)
    for copy in x_copies + y_copies + z_copies:
        copy.wait_send()
    for copy in written:
        copy.wait()


def body(sizes, pop, rbf, owner, slot, comp, ncomp, row):
    _, depth, height, width = pop.shape
    blocks, _, nodes = rbf.shape
    shell = comp.shape[0]
    owners = sizes[1] * sizes[2]
    rows8 = blocks * 8
    any_space = pl.BlockSpec(memory_space=pl.ANY)
    vmem = pl.BlockSpec(memory_space=pltpu.VMEM)
    dma = pltpu.SemaphoreType.DMA
    return pl.pallas_call(
        functools.partial(kernel, sizes),
        out_shape=(
            jax.ShapeDtypeStruct(pop.shape, F32),
            jax.ShapeDtypeStruct((shell, 3, nodes), F32),
            jax.ShapeDtypeStruct((blocks, 3, width), F32),
        ),
        in_specs=[any_space, any_space, vmem, vmem, any_space, any_space, vmem],
        out_specs=(any_space, vmem, vmem),
        scratch_shapes=[
            pltpu.VMEM(pop.shape, F32),
            pltpu.VMEM((4, depth, height, width), F32),
            pltpu.VMEM(pop.shape, F32),
            pltpu.VMEM((3 * depth * height, width), BF16),
            pltpu.VMEM(rbf.shape, BF16),
            pltpu.VMEM(comp.shape, F32),
            pltpu.VMEM(ncomp.shape, F32),
            pltpu.VMEM((rows8, 3 * depth * height), BF16),
            pltpu.VMEM((owners * 32, rows8), BF16),
            pltpu.VMEM((rows8, owners * 32), BF16),
            pltpu.VMEM((rows8, 128), F32),
            pltpu.VMEM((rows8, 128), F32),
            pltpu.VMEM((owners, 32, 128), F32),
            pltpu.VMEM((owners, 32, 128), F32),
            pltpu.VMEM((32, 128), F32),
            pltpu.VMEM((owners, 32, 128), F32),
            pltpu.VMEM((2, height, 128), F32),
            pltpu.VMEM((2, height, 128), F32),
            pltpu.VMEM((2, 5, depth, width), F32),
            pltpu.VMEM((2, 5, depth, width), F32),
            pltpu.VMEM((2, 5, height, width), F32),
            dma((depth,)),
            dma((3,)),
            dma((owners,)),
            dma((owners,)),
            dma((owners,)),
            dma((owners,)),
            dma((4,)),
            dma((4,)),
            dma((2, 5)),
            dma((2, 5)),
            dma((len(NOT_Z) + 20,)),
        ],
        compiler_params=pltpu.CompilerParams(
            collective_id=0, has_side_effects=True, vmem_limit_bytes=48 * 1024 * 1024
        ),
        name="wind_roof_step",
    )(
        pop, rbf, owner.reshape(1, blocks), slot.reshape(1, blocks), comp, ncomp,
        row.reshape(1, blocks),
    )


def solution(mesh):
    sizes = tuple(mesh.shape[name] for name in ("gx", "gy", "gz"))
    return jax.shard_map(
        functools.partial(body, sizes),
        mesh=mesh,
        in_specs=(
            P(None, "gz", "gy", "gx"),
            P(("gx", "gy", "gz"), None, None),
            P(("gx", "gy", "gz"), None),
            P(("gx", "gy", "gz"), None),
            P(("gx", "gy", "gz"), None, None),
            P(("gx", "gy", "gz"), None),
            P(("gx", "gy", "gz")),
        ),
        out_specs=(
            P(None, "gz", "gy", "gx"),
            P(("gx", "gy", "gz"), None, None),
            P(("gx", "gy", "gz"), None, None),
        ),
        check_vma=False,
    )
```

```python
import functools

import jax
import jax.numpy as jnp
from jax import lax
from jax.experimental import pallas as pl
from jax.experimental.pallas import tpu as pltpu
from jax.sharding import PartitionSpec as P

MESH = pl.DeviceIdType.MESH
F32 = jnp.float32
BF16 = jnp.bfloat16
I32 = jnp.int32

lattice_velocity = (
    (0, 0, 0),
    (1, 0, 0),
    (-1, 0, 0),
    (0, 1, 0),
    (0, -1, 0),
    (0, 0, 1),
    (0, 0, -1),
    (1, 1, 0),
    (-1, -1, 0),
    (1, -1, 0),
    (-1, 1, 0),
    (1, 0, 1),
    (-1, 0, -1),
    (1, 0, -1),
    (-1, 0, 1),
    (0, 1, 1),
    (0, -1, -1),
    (0, 1, -1),
    (0, -1, 1),
)
lattice_weight = (1.0 / 3.0,) + (1.0 / 18.0,) * 6 + (1.0 / 36.0,) * 12
load_scale = 30.0
relaxation = 1.6


def moving(component, sign):
    return [q for q in range(19) if lattice_velocity[q][component] == sign]


XP, XM = moving(0, 1), moving(0, -1)
YP, YM = moving(1, 1), moving(1, -1)
ZP, ZM = moving(2, 1), moving(2, -1)
NOT_Z = [q for q in range(19) if lattice_velocity[q][2] == 0]


def iota(shape, dim):
    return lax.broadcasted_iota(I32, shape, dim)


def split(value):
    high = value.astype(BF16)
    low = (value - high.astype(F32)).astype(BF16)
    return high, low


def dot(a, b):
    return jnp.dot(a, b, preferred_element_type=F32)


def kernel(
    sizes,
    pop, rbf, owner_in, slot_in, comp, ncomp, row_in,
    grid, faces, disp, wall,
    owner, slot, row, f, moments, mom, weights, compliance, coupling,
    gather, place, spread, traction, forces, part, recv, mine, shells,
    xs, xr, ys, yr, zr, es, er,
    in_sem, w_sem, ps_sem, pr_sem, ds_sem, dr_sem, hs_sem, hr_sem, zs_sem, zr_sem,
):
    gxn, gyn, gzn = sizes
    owners = gyn * gzn
    depth, height, width = grid.shape[1:]
    blocks = weights.shape[0]
    shell = compliance.shape[0]
    rows8 = blocks * 8
    cells = depth * height
    gx, gy, gz = lax.axis_index("gx"), lax.axis_index("gy"), lax.axis_index("gz")
    me = gy * gzn + gz

    def peer(index):
        return (gx, index // gzn, index % gzn)

    def step(a, n, by):
        return lax.rem(a + by + n, n)

    right = (step(gx, gxn, 1), gy, gz)
    left = (step(gx, gxn, -1), gy, gz)
    north = (gx, step(gy, gyn, 1), gz)
    south = (gx, step(gy, gyn, -1), gz)
    up = (gx, gy, step(gz, gzn, 1))
    down = (gx, gy, step(gz, gzn, -1))

    small = [
        pltpu.make_async_copy(row_in, row, w_sem.at[3]),
        pltpu.make_async_copy(owner_in, owner, w_sem.at[4]),
        pltpu.make_async_copy(slot_in, slot, w_sem.at[5]),
    ]
    for copy in small:
        copy.start()
    loads_in = [pltpu.make_async_copy(pop.at[:, z], f.at[:, z], in_sem.at[z]) for z in range(depth)]
    for copy in loads_in:
        copy.start()
    fixed = [
        pltpu.make_async_copy(rbf, weights, w_sem.at[0]),
        pltpu.make_async_copy(comp, compliance, w_sem.at[1]),
        pltpu.make_async_copy(ncomp, coupling, w_sem.at[2]),
    ]
    for copy in fixed:
        copy.start()

    barrier = pltpu.get_barrier_semaphore()

    def greet(d, carry):
        pl.semaphore_signal(
            barrier, inc=1, device_id=peer(lax.rem(me + d, owners)), device_id_type=MESH
        )
        return carry

    lax.fori_loop(1, owners, greet, 0)
    for item in (left, right):
        pl.semaphore_signal(barrier, inc=1, device_id=item, device_id_type=MESH)

    for copy in small:
        copy.wait()

    square = iota((blocks, blocks), 0) == iota((blocks, blocks), 1)

    def down_rows(ref):
        return jnp.sum(jnp.where(square, ref[...], 0).astype(F32), axis=1, keepdims=True)

    row_s, owner_s, slot_s = down_rows(row), down_rows(owner), down_rows(slot)
    wide = jnp.concatenate(
        [jnp.broadcast_to(item, (blocks, 128)) for item in (row_s, owner_s, slot_s)], axis=1
    ).astype(BF16)
    repeat = (iota((rows8, blocks), 0) // 8 == iota((rows8, blocks), 1)).astype(F32).astype(BF16)
    tall = dot(repeat, wide).astype(I32)
    kind = iota((rows8, 1), 0) % 8
    row_key = tall[:, :128] + kind * cells
    lane = iota((1, 128), 1)
    for j in range(3 * cells // 128):
        hit = row_key == lane + 128 * j
        gather[:, j * 128 : (j + 1) * 128] = hit.astype(F32).astype(BF16)
    target_key = (tall[:, 128:256] * shell + tall[:, 256:]) * 3 + kind
    target_key = jnp.where(kind < 3, target_key, -2)
    for j in range(owners * 32 // 128):
        column = lane + 128 * j
        column_key = jnp.where(column % 32 < 3 * shell, column // 32 * (3 * shell) + column % 32, -1)
        spread[:, j * 128 : (j + 1) * 128] = (target_key == column_key).astype(F32).astype(BF16)
    target_s = ((owner_s * shell + slot_s) * 3).astype(I32)
    across = iota((blocks, rows8), 1)
    lane_key = jnp.sum(
        jnp.where(across // 8 == iota((blocks, rows8), 0), target_s, 0).astype(F32),
        axis=0, keepdims=True,
    ).astype(I32)
    lane_kind = iota((1, rows8), 1) % 8
    lane_key = jnp.where(lane_kind < 3, lane_key + lane_kind, -100)
    place_row = iota((owners * 32, 1), 0)
    place_key = jnp.where(
        place_row % 32 < 3 * shell + 3,
        place_row // 32 * (3 * shell) - 3 + place_row % 32,
        -1000,
    )
    place[...] = (place_key == lane_key).astype(F32).astype(BF16)

    for z in range(depth):
        loads_in[z].wait()

        def moment(c, carry, z=z):
            at = pl.ds(pl.multiple_of(c * 16, 16), 16)
            v = [f[q, z, at, :] for q in range(19)]
            total = v[0]
            for q in range(1, 19):
                total = total + v[q]
            moments[0, z, at, :] = total
            for k in range(3):
                plus, minus = moving(k, 1), moving(k, -1)
                a, b = v[plus[0]], v[minus[0]]
                for q in plus[1:]:
                    a = a + v[q]
                for q in minus[1:]:
                    b = b + v[q]
                m = a - b
                moments[1 + k, z, at, :] = m
                here = pl.ds(pl.multiple_of(k * cells + z * height + c * 16, 16), 16)
                mom[here, :] = (load_scale * m).astype(BF16)
            return carry

        for c in range(height // 16):
            moment(c, 0)

    traction[...] = dot(gather[...], mom[...])
    fixed[0].wait()

    upper = iota((16, 128), 0) < 8

    def force(g, carry):
        for i in range(8):
            at = pl.ds(pl.multiple_of(g * 128 + i * 16, 16), 16)
            pair = traction[at, :]
            pair = jnp.concatenate(
                [jnp.where(upper, pair, 0.0), jnp.where(upper, 0.0, pair)], axis=1
            ).astype(BF16)
            forces[at, :] = dot(pair, weights[pl.ds(g * 16 + i * 2, 2)].reshape(256, 128))
        return carry

    lax.fori_loop(0, blocks // 16, force, 0)
    high, low = split(forces[...])
    both = dot(place[...], jnp.concatenate([high, low], axis=1))
    part[...] = (both[:, :128] + both[:, 128:]).reshape(owners, 32, 128)
    pl.semaphore_wait(barrier, owners - 1 + 2)

    def part_copy(other, mine_at):
        return pltpu.make_async_remote_copy(
            src_ref=part.at[other], dst_ref=recv.at[mine_at],
            send_sem=ps_sem.at[other], recv_sem=pr_sem.at[mine_at],
            device_id=peer(other), device_id_type=MESH,
        )

    def send_part(d, carry):
        part_copy(lax.rem(me + d, owners), me).start()
        return carry

    lax.fori_loop(1, owners, send_part, 0)

    lanes = iota((16, width), 1)

    def collide(z, carry):
        for c in range(height // 16):
            at = pl.ds(c * 16, 16)
            rho = moments[0, z, at, :]
            inverse = 1.0 / rho
            u = [moments[1 + k, z, at, :] * inverse for k in range(3)]
            base = 1.0 - 1.5 * (u[0] * u[0] + u[1] * u[1] + u[2] * u[2])
            scaled = [relaxation * w * rho for w in (1 / 3.0, 1 / 18.0, 1 / 36.0)]
            result = [None] * 19
            result[0] = (1.0 - relaxation) * f[0, z, at, :] + scaled[0] * base
            for q in range(1, 19, 2):
                p = None
                for k in range(3):
                    s = lattice_velocity[q][k]
                    if s:
                        term = u[k]
                        p = (term if s > 0 else -term) if p is None else (p + term if s > 0 else p - term)
                w = scaled[1] if q < 7 else scaled[2]
                even = w * (base + 4.5 * (p * p))
                odd = w * (3.0 * p)
                result[q] = (1.0 - relaxation) * f[q, z, at, :] + (even + odd)
                result[q + 1] = (1.0 - relaxation) * f[q + 1, z, at, :] + (even - odd)
            sent = [xs[0, at, :], xs[1, at, :]]
            for d in range(5):
                here = lanes == d * depth + z
                sent[0] = jnp.where(here, result[XP[d]][:, width - 1 :], sent[0])
                sent[1] = jnp.where(here, result[XM[d]][:, :1], sent[1])
                result[XP[d]] = pltpu.roll(result[XP[d]], 1, 1)
                result[XM[d]] = pltpu.roll(result[XM[d]], width - 1, 1)
            xs[0, at, :] = sent[0]
            xs[1, at, :] = sent[1]
            for q in range(19):
                grid[q, z, at, :] = result[q]
        return carry

    xs[...] = jnp.zeros_like(xs)
    lax.fori_loop(0, depth, collide, 0)

    def halo(src, dst, number, device):
        return pltpu.make_async_remote_copy(
            src_ref=src, dst_ref=dst, send_sem=hs_sem.at[number], recv_sem=hr_sem.at[number],
            device_id=device, device_id_type=MESH,
        )

    x_copies = [halo(xs.at[0], xr.at[0], 0, right), halo(xs.at[1], xr.at[1], 1, left)]
    for copy in x_copies:
        copy.start()

    fixed[1].wait()
    fixed[2].wait()
    comp_high, comp_low = split(compliance[...])
    coup_high, coup_low = split(coupling[...])

    def take_part(d, total):
        other = lax.rem(me + d, owners)
        part_copy(me, other).wait_recv()
        return total + recv[other]

    load = lax.fori_loop(1, owners, take_part, part[me])
    load_high, load_low = split(load)
    aligned = 8 * (shell + 1)
    r8, c8 = iota((aligned, 32), 0), iota((aligned, 32), 1)
    expand = ((r8 % 8 < 3) & (r8 // 8 * 3 + r8 % 8 == c8)).astype(F32).astype(BF16)
    tall_load = dot(expand, jnp.concatenate([load_high, load_low], axis=1))
    moved = []
    for s in range(shell + 1):
        hi = tall_load[s * 8 : s * 8 + 8, :128]
        lo = tall_load[s * 8 : s * 8 + 8, 128:]
        pair = jnp.concatenate([hi, lo], axis=0).astype(BF16)
        first = comp_high[s - 1] if s else coup_high
        second = comp_low[s - 1] if s else coup_low
        a = dot(pair, first)
        b = dot(pair, second)
        moved.append(a[:8] + a[8:] + b[:8])
    moved[1] = moved[1] + moved[0]
    for s in range(shell):
        forces[s * 8 : s * 8 + 8, :] = moved[s + 1]
    for k in range(3):
        disp[k] = forces[pl.ds(k, shell, stride=8), :]
    r8, c8 = iota((32, 8 * shell), 0), iota((32, 8 * shell), 1)
    compact = ((c8 % 8 < 3) & (c8 // 8 * 3 + c8 % 8 == r8)).astype(F32).astype(BF16)
    rounded = jnp.concatenate(moved[1:], axis=0).astype(BF16)
    own = dot(compact, rounded)
    mine[...] = own
    shells[me] = own

    def disp_copy(other, at):
        return pltpu.make_async_remote_copy(
            src_ref=mine, dst_ref=shells.at[at],
            send_sem=ds_sem.at[other], recv_sem=dr_sem.at[at],
            device_id=peer(other), device_id_type=MESH,
        )

    def send_disp(d, carry):
        disp_copy(lax.rem(me + d, owners), me).start()
        return carry

    lax.fori_loop(1, owners, send_disp, 0)

    for copy in x_copies:
        copy.wait_recv()
    for d in range(5):
        for z in range(depth):
            i = d * depth + z
            grid[XP[d], z, :, 0:1] = xr[0, :, i : i + 1]
            grid[XM[d], z, :, width - 1 :] = xr[1, :, i : i + 1]
    for d in range(5):
        ys[0, d] = grid[YP[d], :, height - 1, :]
        ys[1, d] = grid[YM[d], :, 0, :]
    edges = []
    for q in range(15, 19):
        _, along_y, along_z = lattice_velocity[q]
        side, d = (0, YP.index(q)) if along_y > 0 else (1, YM.index(q))
        es[q - 15] = ys[side, d]
        edges.append((q, along_y, along_z, (gx, step(gy, gyn, along_y), step(gz, gzn, along_z))))
    y_copies = [halo(ys.at[0], yr.at[0], 2, north), halo(ys.at[1], yr.at[1], 3, south)]
    for q, along_y, along_z, device in edges:
        line = depth - 1 if along_z > 0 else 0
        es[q - 15, 0:1, :] = es[q - 15, line : line + 1, :]
        y_copies.append(halo(es.at[q - 15], er.at[q - 15], q - 11, device))
    for copy in y_copies:
        copy.start()

    def roll_y(z, carry):
        for d in range(5):
            grid[YP[d], z] = pltpu.roll(grid[YP[d], z], 1, 0)
            grid[YM[d], z] = pltpu.roll(grid[YM[d], z], height - 1, 0)
        return carry

    lax.fori_loop(0, depth, roll_y, 0)
    z_copies = []
    for d in range(5):
        for side, q, z, device in ((0, ZP[d], depth - 1, up), (1, ZM[d], 0, down)):
            z_copies.append(
                pltpu.make_async_remote_copy(
                    src_ref=grid.at[q, z], dst_ref=zr.at[side, d],
                    send_sem=zs_sem.at[side, d], recv_sem=zr_sem.at[side, d],
                    device_id=device, device_id_type=MESH,
                )
            )
            z_copies[-1].start()

    def take_disp(d, carry):
        other = lax.rem(me + d, owners)
        disp_copy(other, other).wait_recv()
        return carry

    lax.fori_loop(1, owners, take_disp, 0)
    everything = shells[...].reshape(owners * 32, 128).astype(BF16)
    traction[...] = dot(spread[...], everything)

    def motion(g, carry):
        for i in range(8):
            at = pl.ds(pl.multiple_of(g * 128 + i * 16, 16), 16)
            value = lax.dot_general(
                traction[at, :].astype(BF16),
                weights[pl.ds(g * 16 + i * 2, 2)].reshape(256, 128),
                (((1,), (1,)), ((), ())), preferred_element_type=F32,
            )
            forces[at, :] = jnp.where(upper, value[:, :128], value[:, 128:])
        return carry

    lax.fori_loop(0, blocks // 16, motion, 0)
    for k in range(3):
        wall[k] = forces[pl.ds(k, blocks, stride=8), :]

    for copy in y_copies:
        copy.wait_recv()
    for d in range(5):
        for side, q, line in ((0, YP[d], 0), (1, YM[d], height - 1)):
            along_z = lattice_velocity[q][2]
            lo, hi = (1 if along_z < 0 else 0), (depth - 1 if along_z > 0 else depth)
            for z in range(lo, hi):
                grid[q, z, line : line + 1, :] = yr[side, d, z : z + 1, :]
    for copy in z_copies:
        copy.wait_recv()
    for d in range(5):
        faces[0, d] = zr[0, d]
        faces[1, d] = zr[1, d]
    for q, along_y, along_z, _ in edges:
        side, d = (0, ZP.index(q)) if along_z > 0 else (1, ZM.index(q))
        line = 0 if along_y > 0 else height - 1
        faces[side, d, line : line + 1, :] = er[q - 15, 0:1, :]

    def drain(d, carry):
        other = lax.rem(me + d, owners)
        part_copy(other, me).wait_send()
        disp_copy(other, me).wait_send()
        return carry

    lax.fori_loop(1, owners, drain, 0)
    for copy in x_copies + y_copies + z_copies:
        copy.wait_send()


def assemble(grid, faces, disp, wall, out, disp_out, wall_out, sem):
    depth = grid.shape[1]
    moves = [(disp, disp_out), (wall, wall_out)]
    for q in NOT_Z:
        moves.append((grid.at[q], out.at[q]))
    for d in range(5):
        moves.append((grid.at[ZP[d], 0 : depth - 1], out.at[ZP[d], 1:depth]))
        moves.append((grid.at[ZM[d], 1:depth], out.at[ZM[d], 0 : depth - 1]))
        moves.append((faces.at[0, d], out.at[ZP[d], 0]))
        moves.append((faces.at[1, d], out.at[ZM[d], depth - 1]))
    copies = [
        pltpu.make_async_copy(src, dst, sem.at[i]) for i, (src, dst) in enumerate(moves)
    ]
    for copy in copies:
        copy.start()
    for copy in copies:
        copy.wait()


def body(sizes, pop, rbf, owner, slot, comp, ncomp, row):
    _, depth, height, width = pop.shape
    blocks, _, nodes = rbf.shape
    shell = comp.shape[0]
    owners = sizes[1] * sizes[2]
    rows8 = blocks * 8
    hbm = pl.BlockSpec(memory_space=pltpu.HBM)
    vmem = pl.BlockSpec(memory_space=pltpu.VMEM)
    dma = pltpu.SemaphoreType.DMA
    disp_shape = jax.ShapeDtypeStruct((3, shell, nodes), F32)
    wall_shape = jax.ShapeDtypeStruct((3, blocks, width), F32)
    parts = pl.pallas_call(
        functools.partial(kernel, sizes),
        out_shape=(
            jax.ShapeDtypeStruct(pop.shape, F32),
            jax.ShapeDtypeStruct((2, 5, height, width), F32),
            disp_shape,
            wall_shape,
        ),
        in_specs=[hbm] * 7,
        out_specs=(vmem,) * 4,
        scratch_shapes=[
            pltpu.VMEM((1, blocks), I32),
            pltpu.VMEM((1, blocks), I32),
            pltpu.VMEM((1, blocks), I32),
            pltpu.VMEM(pop.shape, F32),
            pltpu.VMEM((4, depth, height, width), F32),
            pltpu.VMEM((3 * depth * height, width), BF16),
            pltpu.VMEM(rbf.shape, BF16),
            pltpu.VMEM(comp.shape, F32),
            pltpu.VMEM(ncomp.shape, F32),
            pltpu.VMEM((rows8, 3 * depth * height), BF16),
            pltpu.VMEM((owners * 32, rows8), BF16),
            pltpu.VMEM((rows8, owners * 32), BF16),
            pltpu.VMEM((rows8, 128), F32),
            pltpu.VMEM((rows8, 128), F32),
            pltpu.VMEM((owners, 32, 128), F32),
            pltpu.VMEM((owners, 32, 128), F32),
            pltpu.VMEM((32, 128), F32),
            pltpu.VMEM((owners, 32, 128), F32),
            pltpu.VMEM((2, height, 128), F32),
            pltpu.VMEM((2, height, 128), F32),
            pltpu.VMEM((2, 5, depth, width), F32),
            pltpu.VMEM((2, 5, depth, width), F32),
            pltpu.VMEM((2, 5, height, width), F32),
            pltpu.VMEM((4, depth, width), F32),
            pltpu.VMEM((4, depth, width), F32),
            dma((depth,)),
            dma((6,)),
            dma((owners,)),
            dma((owners,)),
            dma((owners,)),
            dma((owners,)),
            dma((8,)),
            dma((8,)),
            dma((2, 5)),
            dma((2, 5)),
        ],
        compiler_params=pltpu.CompilerParams(
            collective_id=0, has_side_effects=True, vmem_limit_bytes=48 * 1024 * 1024
        ),
        name="wind_roof_step",
    )(
        *(
            pltpu.with_memory_space_constraint(item, pltpu.HBM)
            for item in (
                pop, rbf, owner.reshape(1, blocks), slot.reshape(1, blocks), comp, ncomp,
                row.reshape(1, blocks),
            )
        )
    )
    new, displacement, motion = pl.pallas_call(
        assemble,
        out_shape=(jax.ShapeDtypeStruct(pop.shape, F32), disp_shape, wall_shape),
        in_specs=[vmem] * 4,
        out_specs=(hbm,) * 3,
        scratch_shapes=[dma((2 + len(NOT_Z) + 20,))],
        compiler_params=pltpu.CompilerParams(vmem_limit_bytes=16 * 1024 * 1024),
        name="assemble",
    )(*parts)
    return new, displacement.transpose(1, 0, 2), motion.transpose(1, 0, 2)


def solution(mesh):
    sizes = tuple(mesh.shape[name] for name in ("gx", "gy", "gz"))
    return jax.shard_map(
        functools.partial(body, sizes),
        mesh=mesh,
        in_specs=(
            P(None, "gz", "gy", "gx"),
            P(("gx", "gy", "gz"), None, None),
            P(("gx", "gy", "gz"), None),
            P(("gx", "gy", "gz"), None),
            P(("gx", "gy", "gz"), None, None),
            P(("gx", "gy", "gz"), None),
            P(("gx", "gy", "gz")),
        ),
        out_specs=(
            P(None, "gz", "gy", "gx"),
            P(("gx", "gy", "gz"), None, None),
            P(("gx", "gy", "gz"), None, None),
        ),
        check_vma=False,
    )
```
